32 devices in a mesh: tm: 4 (over y, core), tile: 8 (over z, x).
Axes of the slice: x: 2, y: 2, z: 4, core: 2. Of those that a mesh axis runs over, the one named last changes fastest.
Arguments:
- inputs: bfloat16 [12, 32, 160, 256], P('tm', 'tile'), may hold values from -6 to 6
- grad_out: bfloat16 [12, 32, 160, 256], P('tm', 'tile'), may hold values from -6 to 6
- weight: bfloat16 [3, 3, 3, 256, 256], replicated, may hold values from -0.078125 to 0.078125
- lengths: int32 [8], P('tile'), may hold values from 1 to 4, 24 in all
Outputs:
- grad_in: bfloat16 [12, 32, 160, 256], P('tm', 'tile')
- grad_weight: float32 [3, 3, 3, 256, 256], P(None, None, None, 'tile')
The draws below stay inside these ranges and needn't reach their ends.
Inputs may be any that keep to these rules, and one draw needn't show every extreme that they name: Each tile owns 1 to 4 rows, the lengths sum to 24, and some tile owns exactly 4.
All inputs are finite; a program needn't handle non-finite values. No bound on the sum of `lengths` on one device may be relied on, other than what follows from the above.
Results may differ from the reference program's by a relative error of at most 0.001.
Values may be sent and summed in bfloat16 or wider, within the bound.
A program may use at most 192 MiB of HBM per device.

```python
import math
import jax
import jax.numpy as jnp
import numpy as np
from jax import lax

C = 256
WID = 160
ROWS = 4
FRAMES = 12
HEIGHT = 24
N_TILE = 8


def level_of(own_key, dims, cuts, smallest, top_value):
    factor_of = 1.0
    for dim, parts in cuts:
        heights = jax.random.uniform(jax.random.fold_in(jax.random.fold_in(own_key, 6), dim), (parts,), jnp.float32, smallest / len(cuts), top_value / len(cuts))
        factor_of = factor_of * jnp.repeat(jnp.exp(heights), dims[dim] // parts).reshape((-1,) + (1,) * (len(dims) - 1 - dim))
    return factor_of


def profile(count, total, most, skew):
    weights = [(1 << 20) // math.isqrt(rank ** skew) + 1 for rank in range(2, count + 1)]
    rest, counts = total - most - (count - 1), [1] * (count - 1)
    while rest > 0:
        movable = [i for i in range(count - 1) if counts[i] < most]
        mass, budget = sum([weights[i] for i in movable]), rest
        for i in movable:
            addition = min(most - counts[i], max(1, budget * weights[i] // mass), rest)
            counts[i] = counts[i] + addition
            rest = rest - addition
    return np.array([most] + counts)


def ragged_sizes(stream_key, amount, total, most, lean):
    if amount == 2:
        one = jax.random.randint(stream_key, (), max(1, total - most), min(most, total - 1) + 1)
        return jnp.stack([one, total - one])
    tallies = jnp.asarray(profile(amount, total, most, lean), jnp.int32)
    twos = (amount - 1) // 2
    donor, taker = tallies[1:1 + 2 * twos:2], tallies[2:2 + 2 * twos:2]
    margin = jnp.minimum(donor - 1, most - taker)
    moved = jax.random.randint(jax.random.fold_in(stream_key, 1), (twos,), 0, 1 << 20) % (margin + 1)
    tallies = tallies.at[1:1 + 2 * twos:2].set(donor - moved).at[2:2 + 2 * twos:2].set(taker + moved)
    return tallies[jax.random.permutation(jax.random.fold_in(stream_key, 2), amount)]


def normal_values(key, dims, spread, reach, cuts=(), held_as=jnp.bfloat16):
    factor_of = level_of(key, dims, cuts, -0.22, 0.18) if cuts else 1.0
    entries = jax.random.normal(key, dims, jnp.float32) * spread * factor_of
    return jnp.minimum(jnp.maximum(entries, -reach), reach).astype(held_as)


def setup_inputs(seed: int = 0) -> dict:
    arg_keys = jax.random.split(jax.random.key(seed), 5)
    return {
        "inputs": normal_values(arg_keys[0], (FRAMES, N_TILE * ROWS, WID, C), 1.0, 6.0, ((0, 4), (1, 8))),
        "grad_out": normal_values(arg_keys[1], (FRAMES, N_TILE * ROWS, WID, C), 1.0, 6.0, ((0, 4), (1, 8))),
        "weight": normal_values(arg_keys[2], (3, 3, 3, C, C), (27 * C) ** -0.5, 0.078125),
        "lengths": ragged_sizes(arg_keys[3], N_TILE, HEIGHT, ROWS, 0).astype(jnp.int32),
    }


def reference(inputs, grad_out, weight, lengths):
    offsets = (jnp.cumsum(lengths) - lengths).astype(jnp.int32)
    rows_all = jnp.arange(HEIGHT, dtype=jnp.int32)
    owner = jnp.sum((rows_all[:, None] >= offsets[None, :]).astype(jnp.int32), axis=1) - 1
    source = (owner * ROWS + rows_all - jnp.take(offsets, owner)).astype(jnp.int32)
    x_image = jnp.take(inputs, source, axis=1).astype(jnp.float32)
    g_image = jnp.take(grad_out, source, axis=1).astype(jnp.float32)
    x_padded = jnp.pad(x_image, ((2, 0), (1, 1), (1, 1), (0, 0)))
    g_padded = jnp.pad(g_image, ((0, 2), (1, 1), (1, 1), (0, 0)))
    kernel = weight.astype(jnp.float32)
    grad_image = jnp.zeros(x_image.shape, jnp.float32)
    pieces = []
    for kt in range(3):
        for kh in range(3):
            for kw in range(3):
                x_slice = x_padded[kt:kt + FRAMES, kh:kh + HEIGHT, kw:kw + WID]
                pieces.append(jnp.einsum('fhwc,fhwd->cd', x_slice, g_image, precision=lax.Precision.HIGHEST))
                g_slice = g_padded[2 - kt:2 - kt + FRAMES, 2 - kh:2 - kh + HEIGHT, 2 - kw:2 - kw + WID]
                grad_image = grad_image + jnp.einsum('fhwd,cd->fhwc', g_slice, kernel[kt, kh, kw], precision=lax.Precision.HIGHEST)
    grad_weight = jnp.stack(pieces).reshape(3, 3, 3, C, C)
    slots = jnp.arange(N_TILE * ROWS, dtype=jnp.int32)
    tile_of = (slots // ROWS).astype(jnp.int32)
    within = slots - tile_of * ROWS
    used = within < jnp.take(lengths, tile_of)
    target = jnp.clip(jnp.take(offsets, tile_of) + within, 0, HEIGHT - 1).astype(jnp.int32)
    back = jnp.take(grad_image, target, axis=1)
    grad_in = jnp.where(used[None, :, None, None], back, jnp.zeros_like(back)).astype(jnp.bfloat16)
    return grad_in, grad_weight
```

```python
import functools
import math

import jax
import jax.numpy as jnp
from jax import lax
from jax.experimental import pallas as pl
from jax.experimental.pallas import tpu as pltpu
from jax.sharding import PartitionSpec as P

F32, BF16, I16 = jnp.float32, jnp.bfloat16, jnp.int16
MESH = pl.DeviceIdType.MESH
LANES = 128
GROUPS = 9


def up16(n):
    return -(-n // 16) * 16


def encode(value):
    value = value.reshape(-1, LANES)
    rows = value.shape[0]
    most = jnp.max(jnp.abs(value), axis=0, keepdims=True)
    power = jnp.floor(jnp.log2(jnp.maximum(most, 1e-30))) + 1.0
    parts = [jnp.round(value * (jnp.exp2(-power) * 32000.0))]
    if rows % 16:
        parts.append(jnp.zeros((up16(rows) - rows, LANES), F32))
    parts.append(jnp.broadcast_to(power, (16, LANES)))
    return jnp.concatenate(parts, axis=0).astype(jnp.int32).astype(I16)


def decode(code, shape):
    rows = math.prod(shape) // LANES
    value = code.astype(jnp.int32).astype(F32)
    scale = jnp.exp2(value[-16:-15]) * (1.0 / 32000.0)
    return (value[:rows] * scale).reshape(shape)


def kernel(
    sizes, count_ref, x_ref, g_ref, w_hbm, dx_ref, dw_ref,
    w_ref, own, prev, nxt, last, shifted, patches, x_t, dx_acc, acc, part, done,
    a_out, a_in, x_out, x_in, z_out, z_in, fin,
    w_sem, row_send, row_recv, frame_send, frame_recv, rim_send, rim_recv,
    a_send, a_recv, x_send, x_recv, z_send, z_recv, f_send, f_recv,
):
    n_tm, n_tile, nx, nz, slab, frames, rows, width, chans = sizes
    tm, tile = lax.axis_index("tm"), lax.axis_index("tile")
    core, zi, xi = lax.rem(tm, 2), tile // nx, lax.rem(tile, nx)
    pair = tm + 1 - 2 * core
    behind = lax.rem(tm + n_tm - 1, n_tm)
    plane = rows * width
    count = count_ref[0]

    def copy(src, dst, send, recv, to_tm, to_tile):
        return pltpu.make_async_remote_copy(
            src_ref=src, dst_ref=dst, send_sem=send, recv_sem=recv,
            device_id=(to_tm, to_tile), device_id_type=MESH,
        )

    x_peers = [lax.rem(xi + k, nx) for k in range(1, nx)]
    z_peers = [lax.rem(zi + k, nz) for k in range(1, nz)]
    t_peers = [lax.rem(tm + k, n_tm) for k in range(1, n_tm)]

    load_w = pltpu.make_async_copy(w_hbm, w_ref, w_sem)
    load_w.start()

    barrier = pltpu.get_barrier_semaphore()
    greet = [(tm, lax.rem(tile + 1, n_tile)), (tm, lax.rem(tile + n_tile - 1, n_tile))]
    greet += [(tm, zi * nx + p) for p in x_peers]
    greet += [(tm, p * nx + xi) for p in z_peers]
    greet += [(p, tile) for p in t_peers]
    for who in greet:
        pl.semaphore_signal(barrier, inc=1, device_id=who, device_id_type=MESH)

    last[...] = g_ref[:, pl.ds(lax.rem(count + rows - 1, rows), 1)].reshape(frames, width, chans)
    pl.semaphore_wait(barrier, len(greet))

    first = g_ref.at[:, 0]
    down = copy(last, prev.at[pl.ds(0, frames)], row_send.at[0], row_recv.at[0], tm, lax.rem(tile + 1, n_tile))
    lift = copy(first, nxt.at[pl.ds(0, frames)], row_send.at[1], row_recv.at[1], tm, lax.rem(tile + n_tile - 1, n_tile))
    back = copy(g_ref.at[pl.ds(0, 2)], own, frame_send, frame_recv, behind, tile)
    rims = [
        copy(ref.at[pl.ds(0, 2)], ref.at[pl.ds(frames, 2)], rim_send.at[i], rim_recv.at[i], behind, tile)
        for i, ref in enumerate((prev, nxt))
    ]

    @pl.when(tile < n_tile - 1)
    def _():
        down.start()

    @pl.when(tile > 0)
    def _():
        lift.start()

    @pl.when(tm > 0)
    def _():
        back.start()

    @pl.when(tile == 0)
    def _():
        prev[pl.ds(0, frames)] = jnp.zeros((frames, width, chans), BF16)

    @pl.when(tile == n_tile - 1)
    def _():
        nxt[pl.ds(0, frames)] = jnp.zeros((frames, width, chans), BF16)

    @pl.when(tm == n_tm - 1)
    def _():
        own[...] = jnp.zeros((2, rows, width, chans), BF16)
        prev[pl.ds(frames, 2)] = jnp.zeros((2, width, chans), BF16)
        nxt[pl.ds(frames, 2)] = jnp.zeros((2, width, chans), BF16)

    def spread(row):
        wide = row.astype(F32)
        at = lax.broadcasted_iota(jnp.int32, (width, chans), 0)
        right = jnp.where(at == width - 1, 0.0, pltpu.roll(wide, width - 1, 0)).astype(BF16)
        left = jnp.where(at == 0, 0.0, pltpu.roll(wide, 1, 0)).astype(BF16)
        return jnp.concatenate([right, row, left], axis=-1)

    def center(frame, row, block):
        patches[1, frame, row] = spread(block)

    def rim(frame):
        top = spread(prev[frame])
        shifted[...] = spread(nxt[frame])
        patches[2, frame, 0] = top
        for r in range(1, rows):
            patches[2, frame, r] = patches[1, frame, r - 1]
        for r in range(rows - 1):
            inside = (r + 1 < count).astype(jnp.int32)
            keep = jnp.broadcast_to(inside, (width, 3 * chans)) > 0
            patches[0, frame, r] = jnp.where(
                keep, patches[1, frame, r + 1].astype(F32), shifted[...].astype(F32)
            ).astype(BF16)
        patches[0, frame, rows - 1] = shifted[...]

    def frame_inside(f, _):
        for r in range(rows):
            center(f, r, g_ref[f, r])
        masked = [
            x_ref[f, r].astype(F32) * (r < count).astype(F32) for r in range(rows)
        ]
        x_t[f] = jnp.concatenate(masked, axis=0).T.astype(BF16)
        return 0

    lax.fori_loop(0, frames, frame_inside, 0)

    def rows_arrive():
        @pl.when(tile > 0)
        def _():
            down.wait_recv()

        @pl.when(tile < n_tile - 1)
        def _():
            lift.wait_recv()

        @pl.when(tm > 0)
        def _():
            for r in rims:
                r.start()

        lax.fori_loop(0, frames, lambda f, _: (rim(f), 0)[1], 0)

    def frames_arrive():
        @pl.when(tm < n_tm - 1)
        def _():
            back.wait_recv()
            for r in rims:
                r.wait_recv()

        def one(f, _):
            for r in range(rows):
                center(frames + f, r, own[f, r])
            rim(frames + f)
            return 0

        lax.fori_loop(0, 2, one, 0)

    def taps(g):
        shift, j = g // 3, lax.rem(g, 3)
        return shift, lax.rem(j + 1, 3)

    def grad_w(g):
        shift, kh = taps(g)
        for k in range(3):
            total = None
            for f in range(frames):
                block = patches[kh, shift + f, :, :, k * chans : (k + 1) * chans]
                term = jnp.dot(x_t[f], block.reshape(plane, chans), preferred_element_type=F32)
                total = term if total is None else total + term
            for half in range(2):
                acc[g, 2 * k + half] = total[:, half * LANES : (half + 1) * LANES].reshape(
                    nz, nx, slab, LANES
                )
        a_out[g] = encode(acc[g, pl.ds(3 * (1 - core), 3)])
        send_a(g).start()

    def grad_x(g):
        shift, kh = taps(g)
        kernel_taps = [w_ref[2 - shift, kh, k] for k in range(3)]
        wide = jnp.concatenate(kernel_taps, axis=-1)
        for f in range(frames):
            block = patches[kh, shift + f].reshape(plane, 3 * chans)
            term = lax.dot_general(
                block, wide, (((1,), (1,)), ((), ())), preferred_element_type=F32
            )

            @pl.when(g == 0)
            def _():
                dx_acc[f] = term

            @pl.when(g > 0)
            def _():
                dx_acc[f] = dx_acc[f] + term

    def send_a(g):
        return copy(a_out.at[g], a_in.at[g], a_send.at[g], a_recv.at[g], pair, tile)

    def send_x(g, k):
        return copy(
            x_out.at[g, k], x_in.at[g, k], x_send.at[g, k], x_recv.at[g, k], tm, zi * nx + x_peers[k]
        )

    def send_z(g, k):
        return copy(
            z_out.at[g, k], z_in.at[g, k], z_send.at[g, k], z_recv.at[g, k], tm, z_peers[k] * nx + xi
        )

    def send_f(g, k):
        return copy(
            fin.at[g, tm], fin.at[g, tm], f_send.at[g, k], f_recv.at[g, n_tm - 2 - k], t_peers[k], tile
        )

    def pairs_step(g):
        send_a(g).wait_recv()
        mine = pl.ds(3 * core, 3)
        acc[g, mine] = acc[g, mine] + decode(a_in[g], (3, nz, nx, slab, LANES))
        for k in range(nx - 1):
            x_out[g, k] = encode(acc[g, mine, :, x_peers[k]])
            send_x(g, k).start()

    def x_step(g):
        total = acc[g, pl.ds(3 * core, 3), :, xi]
        for k in range(nx - 1):
            send_x(g, k).wait_recv()
            total = total + decode(x_in[g, k], (3, nz, slab, LANES))
        part[...] = total
        for k in range(nz - 1):
            z_out[g, k] = encode(part[:, z_peers[k]])
            send_z(g, k).start()
        done[g] = part[:, zi]

    def z_step(g):
        total = done[g]
        for k in range(nz - 1):
            send_z(g, k).wait_recv()
            total = total + decode(z_in[g, k], (3, slab, LANES))
        fin[g, tm] = encode(total)
        for k in range(n_tm - 1):
            send_f(g, k).start()

    def final_step(g):
        shift, kh = taps(g)
        for k in range(n_tm - 1):
            pltpu.make_async_remote_copy(
                src_ref=fin.at[g, tm], dst_ref=fin.at[g, t_peers[k]],
                send_sem=f_send.at[g, k], recv_sem=f_recv.at[g, k],
                device_id=(t_peers[k], tile), device_id_type=MESH,
            ).wait_recv()
        for half in range(2):
            total = None
            for y in range(n_tm // 2):
                term = decode(fin[g, 2 * y + half], (3, slab, LANES))
                total = term if total is None else total + term
            for j in range(3):
                lane = 3 * half + j
                at = (lane % 2) * LANES
                dw_ref[2 - shift, kh, lane // 2, :, at : at + LANES] = total[j]

    def step(s, _):
        @pl.when(s == 1)
        def _():
            rows_arrive()

        @pl.when(s == 3)
        def _():
            frames_arrive()

        @pl.when(s < GROUPS)
        def _():
            grad_w(s)

        @pl.when(s == GROUPS)
        def _():
            load_w.wait()

        @pl.when((s >= GROUPS) & (s < 2 * GROUPS))
        def _():
            grad_x(s - GROUPS)

        @pl.when((s >= 1) & (s < 1 + GROUPS))
        def _():
            pairs_step(s - 1)

        for start, act in ((8, final_step), (6, z_step), (4, x_step)):
            @pl.when((s >= start) & (s < start + 2 * GROUPS) & (lax.rem(s, 2) == 0))
            def _():
                act((s - start) // 2)

        return 0

    lax.fori_loop(0, 8 + 2 * GROUPS - 1, step, 0)

    for f in range(frames):
        for r in range(rows):
            used = (r < count).astype(F32)
            dx_ref[f, r] = (dx_acc[f, r * width : (r + 1) * width] * used).astype(BF16)

    @pl.when(tile < n_tile - 1)
    def _():
        down.wait_send()

    @pl.when(tile > 0)
    def _():
        lift.wait_send()

    @pl.when(tm > 0)
    def _():
        back.wait_send()
        for r in rims:
            r.wait_send()

    def drain(g, _):
        send_a(g).wait_send()
        for k in range(nx - 1):
            send_x(g, k).wait_send()
        for k in range(nz - 1):
            send_z(g, k).wait_send()
        for k in range(n_tm - 1):
            send_f(g, k).wait_send()
        return 0

    lax.fori_loop(0, GROUPS, drain, 0)


def body(inputs, grad_out, weight, lengths):
    frames, rows, width, chans = inputs.shape
    n_tm, n_tile = lax.axis_size("tm"), lax.axis_size("tile")
    nx = 2 ** (int(math.log2(n_tile)) // 2)
    nz = n_tile // nx
    slab = chans // n_tile
    sizes = (n_tm, n_tile, nx, nz, slab, frames, rows, width, chans)
    full = frames + 2
    a_rows = 3 * chans + 16
    x_rows = up16(3 * nz * slab) + 16
    z_rows = up16(3 * slab) + 16
    vmem, dma = pltpu.VMEM, pltpu.SemaphoreType.DMA
    flops = 4 * 27 * frames * rows * width * chans * chans
    dx, dw = pl.pallas_call(
        functools.partial(kernel, sizes),
        out_shape=(
            jax.ShapeDtypeStruct((frames, rows, width, chans), BF16),
            jax.ShapeDtypeStruct((3, 3, 3, slab, chans), F32),
        ),
        in_specs=[
            pl.BlockSpec(memory_space=pltpu.SMEM),
            pl.BlockSpec(memory_space=vmem),
            pl.BlockSpec(memory_space=vmem),
            pl.BlockSpec(memory_space=pl.ANY),
        ],
        out_specs=(pl.BlockSpec(memory_space=vmem), pl.BlockSpec(memory_space=vmem)),
        scratch_shapes=[
            vmem((3, 3, 3, chans, chans), BF16),
            vmem((2, rows, width, chans), BF16),
            vmem((full, width, chans), BF16),
            vmem((full, width, chans), BF16),
            vmem((frames, width, chans), BF16),
            vmem((width, 3 * chans), BF16),
            vmem((3, full, rows, width, 3 * chans), BF16),
            vmem((frames, chans, rows * width), BF16),
            vmem((frames, rows * width, chans), F32),
            vmem((GROUPS, 6, nz, nx, slab, LANES), F32),
            vmem((3, nz, slab, LANES), F32),
            vmem((GROUPS, 3, slab, LANES), F32),
            vmem((GROUPS, a_rows, LANES), I16),
            vmem((GROUPS, a_rows, LANES), I16),
            vmem((GROUPS, nx - 1, x_rows, LANES), I16),
            vmem((GROUPS, nx - 1, x_rows, LANES), I16),
            vmem((GROUPS, nz - 1, z_rows, LANES), I16),
            vmem((GROUPS, nz - 1, z_rows, LANES), I16),
            vmem((GROUPS, n_tm, z_rows, LANES), I16),
            dma, dma((2,)), dma((2,)), dma, dma, dma((2,)), dma((2,)),
            dma((GROUPS,)), dma((GROUPS,)),
            dma((GROUPS, nx - 1)), dma((GROUPS, nx - 1)),
            dma((GROUPS, nz - 1)), dma((GROUPS, nz - 1)),
            dma((GROUPS, n_tm - 1)), dma((GROUPS, n_tm - 1)),
        ],
        compiler_params=pltpu.CompilerParams(
            collective_id=0, has_side_effects=True, vmem_limit_bytes=60 * 2**20
        ),
        cost_estimate=pl.CostEstimate(flops=flops, bytes_accessed=8 * 2**20, transcendentals=0),
    )(lengths, inputs, grad_out, weight)
    return dx, dw


def solution(mesh):
    placed = (P("tm", "tile", None, None), P("tm", "tile", None, None), P(), P("tile"))
    return jax.shard_map(
        body,
        mesh=mesh,
        in_specs=placed,
        out_specs=(P("tm", "tile", None, None), P(None, None, None, "tile", None)),
        check_vma=False,
    )
```

```python
import functools
import math

import jax
import jax.numpy as jnp
from jax import lax
from jax.experimental import pallas as pl
from jax.experimental.pallas import tpu as pltpu
from jax.sharding import PartitionSpec as P

F32, BF16, I16 = jnp.float32, jnp.bfloat16, jnp.int16
MESH = pl.DeviceIdType.MESH
LANES = 128
GROUPS = 9


def up16(n):
    return -(-n // 16) * 16


def encode(value):
    value = value.reshape(-1, LANES)
    rows = value.shape[0]
    most = jnp.max(jnp.abs(value), axis=0, keepdims=True)
    power = jnp.floor(jnp.log2(jnp.maximum(most, 1e-30))) + 1.0
    parts = [jnp.round(value * (jnp.exp2(-power) * 32000.0))]
    if rows % 16:
        parts.append(jnp.zeros((up16(rows) - rows, LANES), F32))
    parts.append(jnp.broadcast_to(power, (16, LANES)))
    return jnp.concatenate(parts, axis=0).astype(jnp.int32).astype(I16)


def decode(code, shape):
    rows = math.prod(shape) // LANES
    value = code.astype(jnp.int32).astype(F32)
    scale = jnp.exp2(value[-16:-15]) * (1.0 / 32000.0)
    return (value[:rows] * scale).reshape(shape)


def kernel(
    sizes, count_ref, x_ref, g_ref, w_hbm, dx_ref, dw_ref,
    w_ref, w_t, own, prev, nxt, last, patches, x_t, dx_acc, acc, part, done,
    a_out, a_in, x_out, x_in, z_out, z_in, fin,
    w_sem, row_send, row_recv, frame_send, frame_recv, rim_send, rim_recv,
    a_send, a_recv, x_send, x_recv, z_send, z_recv, f_send, f_recv,
):
    n_tm, n_tile, nx, nz, slab, frames, rows, width, chans = sizes
    tm, tile = lax.axis_index("tm"), lax.axis_index("tile")
    core, zi, xi = lax.rem(tm, 2), tile // nx, lax.rem(tile, nx)
    pair = tm + 1 - 2 * core
    behind = lax.rem(tm + n_tm - 1, n_tm)
    plane = rows * width
    count = count_ref[0]

    def copy(src, dst, send, recv, to_tm, to_tile):
        return pltpu.make_async_remote_copy(
            src_ref=src, dst_ref=dst, send_sem=send, recv_sem=recv,
            device_id=(to_tm, to_tile), device_id_type=MESH,
        )

    x_peers = [lax.rem(xi + k, nx) for k in range(1, nx)]
    z_peers = [lax.rem(zi + k, nz) for k in range(1, nz)]
    t_peers = [lax.rem(tm + k, n_tm) for k in range(1, n_tm)]

    load_w = pltpu.make_async_copy(w_hbm, w_ref, w_sem)
    load_w.start()

    barrier = pltpu.get_barrier_semaphore()
    greet = [(tm, lax.rem(tile + 1, n_tile)), (tm, lax.rem(tile + n_tile - 1, n_tile))]
    greet += [(tm, zi * nx + p) for p in x_peers]
    greet += [(tm, p * nx + xi) for p in z_peers]
    greet += [(p, tile) for p in t_peers]
    for who in greet:
        pl.semaphore_signal(barrier, inc=1, device_id=who, device_id_type=MESH)

    last[...] = g_ref[:, pl.ds(lax.rem(count + rows - 1, rows), 1)].reshape(frames, width, chans)
    pl.semaphore_wait(barrier, len(greet))

    first = g_ref.at[:, 0]
    down = copy(last, prev.at[pl.ds(0, frames)], row_send.at[0], row_recv.at[0], tm, lax.rem(tile + 1, n_tile))
    lift = copy(first, nxt.at[pl.ds(0, frames)], row_send.at[1], row_recv.at[1], tm, lax.rem(tile + n_tile - 1, n_tile))
    back = copy(g_ref.at[pl.ds(0, 2)], own, frame_send, frame_recv, behind, tile)
    rims = [
        copy(ref.at[pl.ds(0, 2)], ref.at[pl.ds(frames, 2)], rim_send.at[i], rim_recv.at[i], behind, tile)
        for i, ref in enumerate((prev, nxt))
    ]

    @pl.when(tile < n_tile - 1)
    def _():
        down.start()

    @pl.when(tile > 0)
    def _():
        lift.start()

    @pl.when(tm > 0)
    def _():
        back.start()

    @pl.when(tile == 0)
    def _():
        prev[pl.ds(0, frames)] = jnp.zeros((frames, width, chans), BF16)

    @pl.when(tile == n_tile - 1)
    def _():
        nxt[pl.ds(0, frames)] = jnp.zeros((frames, width, chans), BF16)

    @pl.when(tm == n_tm - 1)
    def _():
        own[...] = jnp.zeros((2, rows, width, chans), BF16)
        prev[pl.ds(frames, 2)] = jnp.zeros((2, width, chans), BF16)
        nxt[pl.ds(frames, 2)] = jnp.zeros((2, width, chans), BF16)

    def spread(row):
        wide = row.astype(F32)
        at = lax.broadcasted_iota(jnp.int32, (width, chans), 0)
        right = jnp.where(at == width - 1, 0.0, pltpu.roll(wide, width - 1, 0)).astype(BF16)
        left = jnp.where(at == 0, 0.0, pltpu.roll(wide, 1, 0)).astype(BF16)
        return jnp.concatenate([right, row, left], axis=-1)

    def center(frame, row, block):
        patches[frame, row + 1] = spread(block)

    def rim(frame):
        patches[frame, 0] = spread(prev[frame])
        patches[frame, rows + 1] = spread(nxt[frame])
        for r in range(1, rows):
            patches[frame, r + 1] = patches[frame, jnp.where(r < count, r + 1, rows + 1)]

    def frame_inside(f, _):
        for r in range(rows):
            center(f, r, g_ref[f, r])
        masked = [
            x_ref[f, r].astype(F32) * (r < count).astype(F32) for r in range(rows)
        ]
        dx_acc[f] = jnp.zeros((plane, chans), F32)
        x_t[f] = jnp.concatenate(masked, axis=0).T.astype(BF16)
        return 0

    lax.fori_loop(0, frames, frame_inside, 0)

    def rows_arrive():
        @pl.when(tile > 0)
        def _():
            down.wait_recv()

        @pl.when(tile < n_tile - 1)
        def _():
            lift.wait_recv()

        @pl.when(tm > 0)
        def _():
            for r in rims:
                r.start()

        lax.fori_loop(0, frames, lambda f, _: (rim(f), 0)[1], 0)

    def frames_arrive():
        @pl.when(tm < n_tm - 1)
        def _():
            back.wait_recv()
            for r in rims:
                r.wait_recv()

        def one(f, _):
            for r in range(rows):
                center(frames + f, r, own[f, r])
            rim(frames + f)
            return 0

        lax.fori_loop(0, 2, one, 0)

    def taps(g):
        shift, j = g // 3, lax.rem(g, 3)
        return shift, lax.rem(j + 1, 3)

    def grad_w(g):
        shift, kh = taps(g)
        for k in range(3):
            total = None
            for f in range(frames):
                block = patches[shift + f, pl.ds(2 - kh, rows), :, k * chans : (k + 1) * chans]
                term = jnp.dot(x_t[f], block.reshape(plane, chans), preferred_element_type=F32)
                total = term if total is None else total + term
            for half in range(2):
                acc[g, 2 * k + half] = total[:, half * LANES : (half + 1) * LANES].reshape(
                    nz, nx, slab, LANES
                )
        a_out[g] = encode(acc[g, pl.ds(3 * (1 - core), 3)])
        send_a(g).start()

    def grad_x(g):
        shift, kh = taps(g)
        for f in range(frames):
            block = patches[shift + f, pl.ds(2 - kh, rows)].reshape(plane, 3 * chans)
            dx_acc[f] = dx_acc[f] + jnp.dot(
                block, w_t[2 - shift, kh], preferred_element_type=F32
            )

    def turn_w(i, _):
        kt, kh = i // 3, lax.rem(i, 3)
        for k in range(3):
            w_t[kt, kh, k * chans : (k + 1) * chans] = w_ref[kt, kh, k].T
        return 0

    def send_a(g):
        return copy(a_out.at[g], a_in.at[g], a_send.at[g], a_recv.at[g], pair, tile)

    def send_x(g, k):
        return copy(
            x_out.at[g, k], x_in.at[g, k], x_send.at[g, k], x_recv.at[g, k], tm, zi * nx + x_peers[k]
        )

    def send_z(g, k):
        return copy(
            z_out.at[g, k], z_in.at[g, k], z_send.at[g, k], z_recv.at[g, k], tm, z_peers[k] * nx + xi
        )

    def send_f(g, k):
        return copy(
            fin.at[g, tm], fin.at[g, tm], f_send.at[g, k], f_recv.at[g, n_tm - 2 - k], t_peers[k], tile
        )

    def pairs_step(g):
        send_a(g).wait_recv()
        mine = pl.ds(3 * core, 3)
        acc[g, mine] = acc[g, mine] + decode(a_in[g], (3, nz, nx, slab, LANES))
        for k in range(nx - 1):
            x_out[g, k] = encode(acc[g, mine, :, x_peers[k]])
            send_x(g, k).start()

    def x_step(g):
        total = acc[g, pl.ds(3 * core, 3), :, xi]
        for k in range(nx - 1):
            send_x(g, k).wait_recv()
            total = total + decode(x_in[g, k], (3, nz, slab, LANES))
        part[...] = total
        for k in range(nz - 1):
            z_out[g, k] = encode(part[:, z_peers[k]])
            send_z(g, k).start()
        done[g] = part[:, zi]

    def z_step(g):
        total = done[g]
        for k in range(nz - 1):
            send_z(g, k).wait_recv()
            total = total + decode(z_in[g, k], (3, slab, LANES))
        fin[g, tm] = encode(total)
        for k in range(n_tm - 1):
            send_f(g, k).start()

    def final_step(g):
        shift, kh = taps(g)
        for k in range(n_tm - 1):
            pltpu.make_async_remote_copy(
                src_ref=fin.at[g, tm], dst_ref=fin.at[g, t_peers[k]],
                send_sem=f_send.at[g, k], recv_sem=f_recv.at[g, k],
                device_id=(t_peers[k], tile), device_id_type=MESH,
            ).wait_recv()
        for half in range(2):
            total = None
            for y in range(n_tm // 2):
                term = decode(fin[g, 2 * y + half], (3, slab, LANES))
                total = term if total is None else total + term
            for j in range(3):
                lane = 3 * half + j
                at = (lane % 2) * LANES
                dw_ref[2 - shift, kh, lane // 2, :, at : at + LANES] = total[j]

    def step(s, _):
        @pl.when(s == 1)
        def _():
            rows_arrive()

        @pl.when(s == 3)
        def _():
            frames_arrive()

        @pl.when(s < GROUPS)
        def _():
            grad_w(s)

        @pl.when(s == 0)
        def _():
            load_w.wait()
            lax.fori_loop(0, 9, turn_w, 0)

        @pl.when((s < 3) | ((s >= GROUPS) & (s < GROUPS + 6)))
        def _():
            grad_x(s - 6 * (s // GROUPS))

        @pl.when((s >= 1) & (s < 1 + GROUPS))
        def _():
            pairs_step(s - 1)

        for start, act in ((4, x_step), (8, z_step), (12, final_step)):
            @pl.when((s >= start) & (s < start + 2 * GROUPS) & (lax.rem(s, 2) == 0))
            def _():
                act((s - start) // 2)

        return 0

    lax.fori_loop(0, 12 + 2 * GROUPS - 1, step, 0)

    for f in range(frames):
        for r in range(rows):
            used = (r < count).astype(F32)
            dx_ref[f, r] = (dx_acc[f, r * width : (r + 1) * width] * used).astype(BF16)

    @pl.when(tile < n_tile - 1)
    def _():
        down.wait_send()

    @pl.when(tile > 0)
    def _():
        lift.wait_send()

    @pl.when(tm > 0)
    def _():
        back.wait_send()
        for r in rims:
            r.wait_send()

    def drain(g, _):
        send_a(g).wait_send()
        for k in range(nx - 1):
            send_x(g, k).wait_send()
        for k in range(nz - 1):
            send_z(g, k).wait_send()
        for k in range(n_tm - 1):
            send_f(g, k).wait_send()
        return 0

    lax.fori_loop(0, GROUPS, drain, 0)


def body(inputs, grad_out, weight, lengths):
    frames, rows, width, chans = inputs.shape
    n_tm, n_tile = lax.axis_size("tm"), lax.axis_size("tile")
    nx = 2 ** (int(math.log2(n_tile)) // 2)
    nz = n_tile // nx
    slab = chans // n_tile
    sizes = (n_tm, n_tile, nx, nz, slab, frames, rows, width, chans)
    full = frames + 2
    a_rows = 3 * chans + 16
    x_rows = up16(3 * nz * slab) + 16
    z_rows = up16(3 * slab) + 16
    vmem, dma = pltpu.VMEM, pltpu.SemaphoreType.DMA
    flops = 4 * 27 * frames * rows * width * chans * chans
    dx, dw = pl.pallas_call(
        functools.partial(kernel, sizes),
        out_shape=(
            jax.ShapeDtypeStruct((frames, rows, width, chans), BF16),
            jax.ShapeDtypeStruct((3, 3, 3, slab, chans), F32),
        ),
        in_specs=[
            pl.BlockSpec(memory_space=pltpu.SMEM),
            pl.BlockSpec(memory_space=vmem),
            pl.BlockSpec(memory_space=vmem),
            pl.BlockSpec(memory_space=pl.ANY),
        ],
        out_specs=(pl.BlockSpec(memory_space=vmem), pl.BlockSpec(memory_space=vmem)),
        scratch_shapes=[
            vmem((3, 3, 3, chans, chans), BF16),
            vmem((3, 3, 3 * chans, chans), BF16),
            vmem((2, rows, width, chans), BF16),
            vmem((full, width, chans), BF16),
            vmem((full, width, chans), BF16),
            vmem((frames, width, chans), BF16),
            vmem((full, rows + 2, width, 3 * chans), BF16),
            vmem((frames, chans, rows * width), BF16),
            vmem((frames, rows * width, chans), F32),
            vmem((GROUPS, 6, nz, nx, slab, LANES), F32),
            vmem((3, nz, slab, LANES), F32),
            vmem((GROUPS, 3, slab, LANES), F32),
            vmem((GROUPS, a_rows, LANES), I16),
            vmem((GROUPS, a_rows, LANES), I16),
            vmem((GROUPS, nx - 1, x_rows, LANES), I16),
            vmem((GROUPS, nx - 1, x_rows, LANES), I16),
            vmem((GROUPS, nz - 1, z_rows, LANES), I16),
            vmem((GROUPS, nz - 1, z_rows, LANES), I16),
            vmem((GROUPS, n_tm, z_rows, LANES), I16),
            dma, dma((2,)), dma((2,)), dma, dma, dma((2,)), dma((2,)),
            dma((GROUPS,)), dma((GROUPS,)),
            dma((GROUPS, nx - 1)), dma((GROUPS, nx - 1)),
            dma((GROUPS, nz - 1)), dma((GROUPS, nz - 1)),
            dma((GROUPS, n_tm - 1)), dma((GROUPS, n_tm - 1)),
        ],
        compiler_params=pltpu.CompilerParams(
            collective_id=0, has_side_effects=True, vmem_limit_bytes=60 * 2**20
        ),
        cost_estimate=pl.CostEstimate(flops=flops, bytes_accessed=8 * 2**20, transcendentals=0),
    )(lengths, inputs, grad_out, weight)
    return dx, dw


def solution(mesh):
    placed = (P("tm", "tile", None, None), P("tm", "tile", None, None), P(), P("tile"))
    return jax.shard_map(
        body,
        mesh=mesh,
        in_specs=placed,
        out_specs=(P("tm", "tile", None, None), P(None, None, None, "tile", None)),
        check_vma=False,
    )
```

```python
import functools
import math

import jax
import jax.numpy as jnp
from jax import lax
from jax.experimental import pallas as pl
from jax.experimental.pallas import tpu as pltpu
from jax.sharding import PartitionSpec as P

F32, BF16, I16 = jnp.float32, jnp.bfloat16, jnp.int16
MESH = pl.DeviceIdType.MESH
LANES = 128
GROUPS = 9


def up16(n):
    return -(-n // 16) * 16


def encode(value):
    value = value.reshape(-1, LANES)
    rows = value.shape[0]
    most = jnp.max(jnp.abs(value), axis=0, keepdims=True)
    power = jnp.floor(jnp.log2(jnp.maximum(most, 1e-30))) + 1.0
    parts = [jnp.round(value * (jnp.exp2(-power) * 32000.0))]
    if rows % 16:
        parts.append(jnp.zeros((up16(rows) - rows, LANES), F32))
    parts.append(jnp.broadcast_to(power, (16, LANES)))
    return jnp.concatenate(parts, axis=0).astype(jnp.int32).astype(I16)


def decode(code, shape):
    rows = math.prod(shape) // LANES
    value = code.astype(jnp.int32).astype(F32)
    scale = jnp.exp2(value[-16:-15]) * (1.0 / 32000.0)
    return (value[:rows] * scale).reshape(shape)


def kernel(
    sizes, count_ref, x_ref, g_ref, w_hbm, dx_ref, dw_ref,
    w_ref, w_t, own, prev, nxt, last, patches, x_t, dx_acc, acc, part, done,
    a_out, a_in, x_out, x_in, z_out, z_in, fin,
    w_sem, row_send, row_recv, frame_send, frame_recv, rim_send, rim_recv,
    a_send, a_recv, x_send, x_recv, z_send, z_recv, f_send, f_recv,
):
    n_tm, n_tile, nx, nz, slab, frames, rows, width, chans = sizes
    tm, tile = lax.axis_index("tm"), lax.axis_index("tile")
    core, zi, xi = lax.rem(tm, 2), tile // nx, lax.rem(tile, nx)
    pair = tm + 1 - 2 * core
    behind = lax.rem(tm + n_tm - 1, n_tm)
    plane = rows * width
    count = count_ref[0]

    def copy(src, dst, send, recv, to_tm, to_tile):
        return pltpu.make_async_remote_copy(
            src_ref=src, dst_ref=dst, send_sem=send, recv_sem=recv,
            device_id=(to_tm, to_tile), device_id_type=MESH,
        )

    x_peers = [lax.rem(xi + k, nx) for k in range(1, nx)]
    z_peers = [lax.rem(zi + k, nz) for k in range(1, nz)]
    t_peers = [lax.rem(tm + k, n_tm) for k in range(1, n_tm)]

    load_w = pltpu.make_async_copy(w_hbm, w_ref, w_sem)
    load_w.start()

    barrier = pltpu.get_barrier_semaphore()
    greet = [(tm, lax.rem(tile + 1, n_tile)), (tm, lax.rem(tile + n_tile - 1, n_tile))]
    greet += [(tm, zi * nx + p) for p in x_peers]
    greet += [(tm, p * nx + xi) for p in z_peers]
    greet += [(p, tile) for p in t_peers]
    for who in greet:
        pl.semaphore_signal(barrier, inc=1, device_id=who, device_id_type=MESH)

    last[...] = g_ref[:, pl.ds(lax.rem(count + rows - 1, rows), 1)].reshape(frames, width, chans)
    pl.semaphore_wait(barrier, len(greet))

    first = g_ref.at[:, 0]
    down = copy(last, prev.at[pl.ds(0, frames)], row_send.at[0], row_recv.at[0], tm, lax.rem(tile + 1, n_tile))
    lift = copy(first, nxt.at[pl.ds(0, frames)], row_send.at[1], row_recv.at[1], tm, lax.rem(tile + n_tile - 1, n_tile))
    back = copy(g_ref.at[pl.ds(0, 2)], own, frame_send, frame_recv, behind, tile)
    rims = [
        copy(ref.at[pl.ds(0, 2)], ref.at[pl.ds(frames, 2)], rim_send.at[i], rim_recv.at[i], behind, tile)
        for i, ref in enumerate((prev, nxt))
    ]

    @pl.when(tile < n_tile - 1)
    def _():
        down.start()

    @pl.when(tile > 0)
    def _():
        lift.start()

    @pl.when(tm > 0)
    def _():
        back.start()

    @pl.when(tile == 0)
    def _():
        prev[pl.ds(0, frames)] = jnp.zeros((frames, width, chans), BF16)

    @pl.when(tile == n_tile - 1)
    def _():
        nxt[pl.ds(0, frames)] = jnp.zeros((frames, width, chans), BF16)

    @pl.when(tm == n_tm - 1)
    def _():
        own[...] = jnp.zeros((2, rows, width, chans), BF16)
        prev[pl.ds(frames, 2)] = jnp.zeros((2, width, chans), BF16)
        nxt[pl.ds(frames, 2)] = jnp.zeros((2, width, chans), BF16)

    def spread(row):
        wide = row.astype(F32)
        at = lax.broadcasted_iota(jnp.int32, (width, chans), 0)
        right = jnp.where(at == width - 1, 0.0, pltpu.roll(wide, width - 1, 0)).astype(BF16)
        left = jnp.where(at == 0, 0.0, pltpu.roll(wide, 1, 0)).astype(BF16)
        return jnp.concatenate([right, row, left], axis=-1)

    def center(frame, row, block):
        patches[frame, row + 1] = spread(block)

    def rim(frame):
        patches[frame, 0] = spread(prev[frame])
        patches[frame, rows + 1] = spread(nxt[frame])
        for r in range(1, rows):
            patches[frame, r + 1] = patches[frame, jnp.where(r < count, r + 1, rows + 1)]

    def frame_inside(f, _):
        for r in range(rows):
            center(f, r, g_ref[f, r])
        masked = [
            x_ref[f, r].astype(F32) * (r < count).astype(F32) for r in range(rows)
        ]
        dx_acc[f] = jnp.zeros((plane, chans), F32)
        x_t[f] = jnp.concatenate(masked, axis=0).T.astype(BF16)
        return 0

    lax.fori_loop(0, frames, frame_inside, 0)

    def rows_arrive():
        @pl.when(tile > 0)
        def _():
            down.wait_recv()

        @pl.when(tile < n_tile - 1)
        def _():
            lift.wait_recv()

        @pl.when(tm > 0)
        def _():
            for r in rims:
                r.start()

        lax.fori_loop(0, frames, lambda f, _: (rim(f), 0)[1], 0)

    def frames_arrive():
        @pl.when(tm < n_tm - 1)
        def _():
            back.wait_recv()
            for r in rims:
                r.wait_recv()

        def one(f, _):
            for r in range(rows):
                center(frames + f, r, own[f, r])
            rim(frames + f)
            return 0

        lax.fori_loop(0, 2, one, 0)

    def taps(g):
        shift, j = g // 3, lax.rem(g, 3)
        return shift, lax.rem(j + 1, 3)

    def grad_w(g):
        shift, kh = taps(g)
        for k in range(3):
            total = None
            for f in range(frames):
                block = patches[shift + f, pl.ds(2 - kh, rows), :, k * chans : (k + 1) * chans]
                term = jnp.dot(x_t[f], block.reshape(plane, chans), preferred_element_type=F32)
                total = term if total is None else total + term
            for half in range(2):
                acc[g, 2 * k + half] = total[:, half * LANES : (half + 1) * LANES].reshape(
                    nz, nx, slab, LANES
                )
        a_out[g] = encode(acc[g, pl.ds(3 * (1 - core), 3)])
        send_a(g).start()

    def grad_x(g):
        shift, kh = taps(g)
        for f in range(frames):
            block = patches[shift + f, pl.ds(2 - kh, rows)].reshape(plane, 3 * chans)
            dx_acc[f] = dx_acc[f] + jnp.dot(
                block, w_t[2 - shift, kh], preferred_element_type=F32
            )

    def turn_w(i, _):
        kt, kh = i // 3, lax.rem(i, 3)
        for k in range(3):
            w_t[kt, kh, k * chans : (k + 1) * chans] = w_ref[kt, kh, k].T
        return 0

    def send_a(g):
        return copy(a_out.at[g], a_in.at[g], a_send.at[g], a_recv.at[g], pair, tile)

    def send_x(g, k):
        return copy(
            x_out.at[g, k], x_in.at[g, k], x_send.at[g, k], x_recv.at[g, k], tm, zi * nx + x_peers[k]
        )

    def send_z(g, k):
        return copy(
            z_out.at[g, k], z_in.at[g, k], z_send.at[g, k], z_recv.at[g, k], tm, z_peers[k] * nx + xi
        )

    def send_f(g, k):
        return copy(
            fin.at[g, tm], fin.at[g, tm], f_send.at[g, k], f_recv.at[g, n_tm - 2 - k], t_peers[k], tile
        )

    def pairs_step(g):
        send_a(g).wait_recv()
        mine = pl.ds(3 * core, 3)
        acc[g, mine] = acc[g, mine] + decode(a_in[g], (3, nz, nx, slab, LANES))
        for k in range(nx - 1):
            x_out[g, k] = encode(acc[g, mine, :, x_peers[k]])
            send_x(g, k).start()

    def x_step(g):
        total = acc[g, pl.ds(3 * core, 3), :, xi]
        for k in range(nx - 1):
            send_x(g, k).wait_recv()
            total = total + decode(x_in[g, k], (3, nz, slab, LANES))
        part[...] = total
        for k in range(nz - 1):
            z_out[g, k] = encode(part[:, z_peers[k]])
            send_z(g, k).start()
        done[g] = part[:, zi]

    def z_step(g):
        total = done[g]
        for k in range(nz - 1):
            send_z(g, k).wait_recv()
            total = total + decode(z_in[g, k], (3, slab, LANES))
        fin[g, tm] = encode(total)
        for k in range(n_tm - 1):
            send_f(g, k).start()

    def final_step(g):
        shift, kh = taps(g)
        for k in range(n_tm - 1):
            pltpu.make_async_remote_copy(
                src_ref=fin.at[g, tm], dst_ref=fin.at[g, t_peers[k]],
                send_sem=f_send.at[g, k], recv_sem=f_recv.at[g, k],
                device_id=(t_peers[k], tile), device_id_type=MESH,
            ).wait_recv()
        for half in range(2):
            total = None
            for y in range(n_tm // 2):
                term = decode(fin[g, 2 * y + half], (3, slab, LANES))
                total = term if total is None else total + term
            for j in range(3):
                lane = 3 * half + j
                at = (lane % 2) * LANES
                dw_ref[2 - shift, kh, lane // 2, :, at : at + LANES] = total[j]

    def step(s, _):
        @pl.when(s == 1)
        def _():
            rows_arrive()

        @pl.when(s == 5)
        def _():
            frames_arrive()

        @pl.when((s < 3) | ((s >= 5) & (s < 11)))
        def _():
            grad_w(s - 2 * ((s + 3) // 8))

        @pl.when(s == 0)
        def _():
            load_w.wait()
            lax.fori_loop(0, 9, turn_w, 0)

        @pl.when((s < 3) | ((s >= 11) & (s < 17)))
        def _():
            grad_x(s - 8 * ((s + 5) // 16))

        for act, early, late, pace in (
            (pairs_step, 1, 6, 1), (x_step, 2, 8, 2), (z_step, 6, 12, 2), (final_step, 8, 16, 2)
        ):
            @pl.when((s >= early) & (s < early + 3))
            def _():
                act(s - early)

            @pl.when((s >= late) & (s < late + 6 * pace) & (lax.rem(s - late + 60, pace) == 0))
            def _():
                act(3 + (s - late) // pace)

        return 0

    lax.fori_loop(0, 27, step, 0)

    for f in range(frames):
        for r in range(rows):
            used = (r < count).astype(F32)
            dx_ref[f, r] = (dx_acc[f, r * width : (r + 1) * width] * used).astype(BF16)

    @pl.when(tile < n_tile - 1)
    def _():
        down.wait_send()

    @pl.when(tile > 0)
    def _():
        lift.wait_send()

    @pl.when(tm > 0)
    def _():
        back.wait_send()
        for r in rims:
            r.wait_send()

    def drain(g, _):
        send_a(g).wait_send()
        for k in range(nx - 1):
            send_x(g, k).wait_send()
        for k in range(nz - 1):
            send_z(g, k).wait_send()
        for k in range(n_tm - 1):
            send_f(g, k).wait_send()
        return 0

    lax.fori_loop(0, GROUPS, drain, 0)


def body(inputs, grad_out, weight, lengths):
    frames, rows, width, chans = inputs.shape
    n_tm, n_tile = lax.axis_size("tm"), lax.axis_size("tile")
    nx = 2 ** (int(math.log2(n_tile)) // 2)
    nz = n_tile // nx
    slab = chans // n_tile
    sizes = (n_tm, n_tile, nx, nz, slab, frames, rows, width, chans)
    full = frames + 2
    a_rows = 3 * chans + 16
    x_rows = up16(3 * nz * slab) + 16
    z_rows = up16(3 * slab) + 16
    vmem, dma = pltpu.VMEM, pltpu.SemaphoreType.DMA
    flops = 4 * 27 * frames * rows * width * chans * chans
    dx, dw = pl.pallas_call(
        functools.partial(kernel, sizes),
        out_shape=(
            jax.ShapeDtypeStruct((frames, rows, width, chans), BF16),
            jax.ShapeDtypeStruct((3, 3, 3, slab, chans), F32),
        ),
        in_specs=[
            pl.BlockSpec(memory_space=pltpu.SMEM),
            pl.BlockSpec(memory_space=vmem),
            pl.BlockSpec(memory_space=vmem),
            pl.BlockSpec(memory_space=pl.ANY),
        ],
        out_specs=(pl.BlockSpec(memory_space=vmem), pl.BlockSpec(memory_space=vmem)),
        scratch_shapes=[
            vmem((3, 3, 3, chans, chans), BF16),
            vmem((3, 3, 3 * chans, chans), BF16),
            vmem((2, rows, width, chans), BF16),
            vmem((full, width, chans), BF16),
            vmem((full, width, chans), BF16),
            vmem((frames, width, chans), BF16),
            vmem((full, rows + 2, width, 3 * chans), BF16),
            vmem((frames, chans, rows * width), BF16),
            vmem((frames, rows * width, chans), F32),
            vmem((GROUPS, 6, nz, nx, slab, LANES), F32),
            vmem((3, nz, slab, LANES), F32),
            vmem((GROUPS, 3, slab, LANES), F32),
            vmem((GROUPS, a_rows, LANES), I16),
            vmem((GROUPS, a_rows, LANES), I16),
            vmem((GROUPS, nx - 1, x_rows, LANES), I16),
            vmem((GROUPS, nx - 1, x_rows, LANES), I16),
            vmem((GROUPS, nz - 1, z_rows, LANES), I16),
            vmem((GROUPS, nz - 1, z_rows, LANES), I16),
            vmem((GROUPS, n_tm, z_rows, LANES), I16),
            dma, dma((2,)), dma((2,)), dma, dma, dma((2,)), dma((2,)),
            dma((GROUPS,)), dma((GROUPS,)),
            dma((GROUPS, nx - 1)), dma((GROUPS, nx - 1)),
            dma((GROUPS, nz - 1)), dma((GROUPS, nz - 1)),
            dma((GROUPS, n_tm - 1)), dma((GROUPS, n_tm - 1)),
        ],
        compiler_params=pltpu.CompilerParams(
            collective_id=0, has_side_effects=True, vmem_limit_bytes=60 * 2**20
        ),
        cost_estimate=pl.CostEstimate(flops=flops, bytes_accessed=8 * 2**20, transcendentals=0),
    )(lengths, inputs, grad_out, weight)
    return dx, dw


def solution(mesh):
    placed = (P("tm", "tile", None, None), P("tm", "tile", None, None), P(), P("tile"))
    return jax.shard_map(
        body,
        mesh=mesh,
        in_specs=placed,
        out_specs=(P("tm", "tile", None, None), P(None, None, None, "tile", None)),
        check_vma=False,
    )
```
